256 devices in a mesh: replica: 8 (over x_lo, y), fsdp: 32 (over z, x_hi, core).
Axes of the slice: x: 4 (x_hi: 2, x_lo: 2; x = x_hi * 2 + x_lo), y: 4, z: 8, core: 2. Of those that a mesh axis runs over, the one named last changes fastest.
Arguments:
- activations: bfloat16 [32768, 12288], P(('replica', 'fsdp')), may hold values from -24 to 24
- inner_weight: bfloat16 [8, 12288, 1024], P('replica', 'fsdp'), may hold values from -0.0546875 to 0.0546875
- out_cotangent: bfloat16 [32768, 1024], P(('replica', 'fsdp')), may hold values from -0.059814453 to 0.059814453
- local_fragment: bfloat16 [8, 512, 12288], P('replica', None, 'fsdp'), may hold values from -6 to 6
- outer_base: float32 [512, 12288], P('replica', 'fsdp'), may hold values from -6 to 6
- outer_momentum: float32 [512, 12288], P('replica', 'fsdp'), may hold values from -3 to 3
Outputs:
- inner_grad: float32 [8, 12288, 1024], P('replica', 'fsdp')
- new_base: float32 [512, 12288], P('replica', 'fsdp')
- new_momentum: float32 [512, 12288], P('replica', 'fsdp')
- merged_fragment: bfloat16 [8, 512, 12288], P('replica', None, 'fsdp')
The draws below stay inside these ranges and needn't reach their ends.
All inputs are finite; a program needn't handle non-finite values.
Results may differ from the reference program's by a relative error of at most 0.012.
Values may be sent and summed in bfloat16 or wider, within the bound.
No kernel may reach another device: no remote copies, remote signals or barrier semaphores. Data moves between devices by JAX's collectives and lax.ppermute only.
A program may use at most 128 MiB of HBM per device.

```python
import jax
import jax.numpy as jnp
from jax import lax

D = 12288
HID = 1024
HEAD = 128
TOK_DEV = 128
FRAG_ROWS = 512
REPLICAS = 8
TOKENS = 32768
N_REPLICA = 8
N_FSDP = 32


def spiked(entries, stream_key, source, target, parts, factor):
    def block_of(position):
        return (jnp.arange(entries.shape[position]) // (entries.shape[position] // parts)).reshape((-1,) + (1,) * (entries.ndim - 1 - position))

    first = jax.random.permutation(stream_key, parts)[block_of(target)]
    second = (block_of(target) + parts // 2) % parts
    return jnp.where((block_of(source) == first) | (block_of(source) == second), factor * entries, entries)


def steps_of(rng, extent, cuts, low, largest):
    factor_of, own = 1.0, jax.random.fold_in(rng, 6)
    for axis_at, blocks in cuts:
        heights = jnp.exp(jax.random.uniform(jax.random.fold_in(own, axis_at), (blocks,), jnp.float32, low / len(cuts), largest / len(cuts)))
        factor_of = factor_of * jnp.repeat(heights, extent[axis_at] // blocks).reshape([-1 if axis == axis_at else 1 for axis in range(len(extent))])
    return factor_of


def bell_draw(stream_key, dims, spread, reach, pieces=(), dtype=jnp.bfloat16):
    result = spread * jax.random.normal(stream_key, dims, jnp.float32)
    if pieces:
        result = result * steps_of(stream_key, dims, pieces, -0.22, 0.18)
    return jnp.clip(result, -reach, reach).astype(dtype)


def bell_draw_with(stream_key, extent, spread, limit, pieces, heavy, dtype=jnp.bfloat16):
    array = spread * jax.random.normal(stream_key, extent, jnp.float32)
    if pieces:
        array = array * steps_of(stream_key, extent, pieces, -0.22, 0.18)
    return jnp.clip(spiked(array, jax.random.fold_in(stream_key, 3), *heavy), -limit, limit).astype(dtype)


def setup_inputs(seed: int = 0) -> dict:
    splits = jax.random.split(jax.random.key(seed), 7)
    activations = bell_draw_with(splits[0], (TOKENS, D), 1.0, 24.0, ((0, 256),), (0, 1, 256, 6.0))
    inner_weight = bell_draw(splits[1], (REPLICAS, D, HID), D ** -0.5, 0.0546875, ((0, 8), (1, 32)))
    out_cotangent = bell_draw(splits[2], (TOKENS, HID), 0.01, 0.059814453, ((0, 256),))
    local_fragment = bell_draw(splits[3], (REPLICAS, FRAG_ROWS, D), 1.0, 6.0, ((0, 8), (2, 32)))
    outer_base = bell_draw(splits[4], (FRAG_ROWS, D), 1.0, 6.0, ((0, 8), (1, 32)), jnp.float32)
    outer_momentum = bell_draw(splits[5], (FRAG_ROWS, D), 0.5, 3.0, ((0, 8), (1, 32)), jnp.float32)
    return {"activations": activations, "inner_weight": inner_weight, "out_cotangent": out_cotangent, "local_fragment": local_fragment, "outer_base": outer_base, "outer_momentum": outer_momentum}


def norm_slope(pre, cotangent):
    heads = pre.reshape(pre.shape[0], pre.shape[1] // HEAD, HEAD)
    upstream = cotangent.astype(jnp.float32).reshape(heads.shape)
    inverse = lax.rsqrt(lax.optimization_barrier(jnp.mean(heads * heads, axis=-1, keepdims=True)) + 1e-06)
    normed = heads * inverse
    along = lax.optimization_barrier(jnp.mean(upstream * normed, axis=-1, keepdims=True))
    return ((upstream - normed * along) * inverse).reshape(pre.shape).astype(jnp.bfloat16)

def inner_one(triple):
    rows, weight, cotangent = triple
    pre = jnp.dot(rows, weight, preferred_element_type=jnp.float32)
    slope = norm_slope(pre, cotangent)
    return lax.dot_general(rows, slope, (((0,), (0,)), ((), ())), preferred_element_type=jnp.float32)

def reference(activations, inner_weight, out_cotangent, local_fragment, outer_base, outer_momentum):
    rows = activations.reshape(N_REPLICA, N_FSDP * TOK_DEV, D)
    cotangent = out_cotangent.reshape(N_REPLICA, N_FSDP * TOK_DEV, HID)
    inner_grad = lax.map(inner_one, (rows, inner_weight, cotangent))
    local_wide = local_fragment.astype(jnp.float32)
    average = lax.optimization_barrier(jnp.sum(local_wide, axis=0)) / N_REPLICA
    delta = outer_base - average
    new_momentum = 0.9 * outer_momentum + delta
    new_base = outer_base - 0.7 * (delta + 0.9 * new_momentum)
    base_half = new_base.astype(jnp.bfloat16)
    merged = (0.5 * base_half.astype(jnp.float32)[None] + 0.5 * local_wide).astype(jnp.bfloat16)
    return (inner_grad, new_base, new_momentum, merged)
```

```python
import jax
import jax.numpy as jnp
from jax import lax
from jax.experimental import pallas as pl
from jax.experimental.pallas import tpu as pltpu
from jax.sharding import Mesh, PartitionSpec as P

HEAD = 128
EDGES = (0, 640, 1024)
F32, BF16 = jnp.float32, jnp.bfloat16
RIGHT = [(i, (i + 1) % 8) for i in range(8)]
LEFT = [(i, (i + 7) % 8) for i in range(8)]
SWAP = [(0, 1), (1, 0)]
BOTH = [(0, 3), (1, 2), (2, 1), (3, 0)]
FAR = [(0, 2), (1, 3), (2, 0), (3, 1)]
NEAR = [(0, 1), (1, 0), (2, 3), (3, 2)]


def norm_slope(pre, cotangent):
    heads = pre.reshape(pre.shape[0], pre.shape[1] // HEAD, HEAD)
    upstream = cotangent.astype(F32).reshape(heads.shape)
    inverse = lax.rsqrt(jnp.mean(heads * heads, axis=-1, keepdims=True) + 1e-06)
    normed = heads * inverse
    along = jnp.mean(upstream * normed, axis=-1, keepdims=True)
    return ((upstream - normed * along) * inverse).reshape(pre.shape).astype(BF16)


def split_columns(rows, mine):
    tokens, width = rows.shape[0], rows.shape[1] // 32

    def kernel(mine_ref, rows_ref, o0, o1, o2, o3, sems):
        copies = []
        for k, out in ((3, o3), (2, o2), (1, o1), (0, o0)):
            member = mine_ref[0] ^ k
            for z in range(8):
                start = pl.multiple_of((4 * z + member) * width, width)
                copies.append(
                    pltpu.make_async_copy(
                        rows_ref.at[:, pl.ds(start, width)], out.at[z], sems.at[k, z]
                    )
                )
                copies[-1].start()
        for copy in copies:
            copy.wait()

    return pl.pallas_call(
        kernel,
        in_specs=[pl.BlockSpec(memory_space=pltpu.SMEM), pl.BlockSpec(memory_space=pl.ANY)],
        out_specs=[pl.BlockSpec(memory_space=pltpu.VMEM)] * 4,
        out_shape=[jax.ShapeDtypeStruct((8, tokens, width), rows.dtype)] * 4,
        scratch_shapes=[pltpu.SemaphoreType.DMA((4, 8))],
        compiler_params=pltpu.CompilerParams(vmem_limit_bytes=16 << 20),
    )(mine.reshape(1), rows)


def gather_ring(shard):
    half = shard.shape[0] // 2
    whole = slice(0, shard.shape[0])
    from_left = from_right = shard
    found = [(0, whole, shard)]
    for step in range(1, 4):
        from_left = lax.ppermute(from_left, "z", RIGHT)
        from_right = lax.ppermute(from_right, "z", LEFT)
        found += [(-step, whole, from_left), (step, whole, from_right)]
    found.append((4, slice(0, half), lax.ppermute(from_left[:half], "z", RIGHT)))
    found.append((4, slice(half, None), lax.ppermute(from_right[half:], "z", LEFT)))
    return found


def scatter_ring(part_of):
    def plus(part, arrived):
        return (part + arrived.astype(F32)).astype(BF16)

    far = part_of(4).astype(BF16)
    half = far.shape[0] // 2
    up = lax.ppermute(far[:half], "z", RIGHT)
    down = lax.ppermute(far[half:], "z", LEFT)
    ahead, behind = part_of(3), part_of(-3)
    up = jnp.concatenate([plus(ahead[:half], up), ahead[half:].astype(BF16)])
    down = jnp.concatenate([behind[:half].astype(BF16), plus(behind[half:], down)])
    for d in (2, 1):
        up = lax.ppermute(up, "z", RIGHT)
        down = lax.ppermute(down, "z", LEFT)
        up, down = plus(part_of(d), up), plus(part_of(-d), down)
    up = lax.ppermute(up, "z", RIGHT)
    down = lax.ppermute(down, "z", LEFT)
    return part_of(0) + up.astype(F32) + down.astype(F32)


def merge(fragment, base, momentum):
    rows = base.shape[0]
    stages = (("xl", SWAP, lax.axis_index("xl")), ("y", FAR, lax.axis_index("y") // 2), ("y", NEAR, lax.axis_index("y") % 2))
    total = fragment
    for axis, moves, bit in stages:
        half = total.shape[0] // 2
        kept = lax.dynamic_slice_in_dim(total, bit * half, half, 0)
        sent = lax.dynamic_slice_in_dim(total, (1 - bit) * half, half, 0)
        total = kept.astype(F32) + lax.ppermute(sent, axis, moves).astype(F32)
    delta = base - total / 8
    new_momentum = 0.9 * momentum + delta
    new_base = base - 0.7 * (delta + 0.9 * new_momentum)
    half_base = new_base.astype(BF16)
    for axis, moves, bit in stages[::-1]:
        other = lax.ppermute(half_base, axis, moves)
        both = jnp.concatenate([half_base, other, half_base])
        half_base = lax.dynamic_slice_in_dim(both, bit * half_base.shape[0], 2 * half_base.shape[0], 0)
    merged = (0.5 * half_base.astype(F32) + 0.5 * fragment.astype(F32)).astype(BF16)
    return new_base, new_momentum, merged


def exchange(parts):
    return [
        parts[0],
        lax.ppermute(parts[1], "c", SWAP),
        lax.ppermute(parts[2], "xh", SWAP),
        lax.ppermute(parts[3], ("xh", "c"), BOTH),
    ]


def body(activations, inner_weight, out_cotangent, local_fragment, outer_base, outer_momentum):
    weight = inner_weight[0]
    z = lax.axis_index("z")
    mine = lax.axis_index("xh") * 2 + lax.axis_index("c")
    cuts = [slice(a, b) for a, b in zip(EDGES[:-1], EDGES[1:])]
    weights = [weight[:, cut] for cut in cuts]

    columns = jnp.concatenate(exchange(split_columns(activations, mine)), axis=1)

    def block(d):
        return lax.dynamic_index_in_dim(columns, (z + d) % 8, 0, keepdims=False)

    grads = []
    for i, cut in enumerate(cuts):
        found = gather_ring(weights[i])
        if i + 1 < len(cuts):
            weights[i + 1], _ = lax.optimization_barrier((weights[i + 1], found[-4][2]))
        if i == 0:
            local_fragment, _ = lax.optimization_barrier((local_fragment, found[1][2]))
        pre = 0.0
        for d, rows, piece in found:
            pre = pre + jnp.dot(block(d)[:, rows], piece, preferred_element_type=F32)
        own, *others = [pre[128 * k : 128 * (k + 1)] for k in range(4)]
        for part in exchange([own] + [part.astype(BF16) for part in others])[1:]:
            own = own + part.astype(F32)
        slope = norm_slope(own, out_cotangent[:, cut])
        slopes = jnp.concatenate(exchange([slope] * 4))

        def part_of(d, slopes=slopes):
            return lax.dot_general(block(d), slopes, (((0,), (0,)), ((), ())), preferred_element_type=F32)

        grads.append(scatter_ring(part_of))
    new_base, new_momentum, merged = merge(local_fragment[0], outer_base, outer_momentum)
    return (jnp.concatenate(grads, axis=1)[None], new_base, new_momentum, merged[None])


def solution(mesh):
    axes = ("xl", "y", "z", "xh", "c")
    mesh = Mesh(mesh.devices.reshape(2, 4, 8, 2, 2), axes)
    replica, fsdp = ("xl", "y"), ("z", "xh", "c")
    placed = (
        P(axes, None),
        P(replica, fsdp, None),
        P(axes, None),
        P(replica, None, fsdp),
        P(replica, fsdp),
        P(replica, fsdp),
    )
    return jax.shard_map(
        body,
        mesh=mesh,
        in_specs=placed,
        out_specs=(
            P(replica, fsdp, None),
            P(replica, fsdp),
            P(replica, fsdp),
            P(replica, None, fsdp),
        ),
        check_vma=False,
    )
```

```python
import jax
import jax.numpy as jnp
from jax import lax
from jax.experimental import pallas as pl
from jax.experimental.pallas import tpu as pltpu
from jax.sharding import Mesh, PartitionSpec as P

HEAD = 128
CUTS = 2
F32, BF16 = jnp.float32, jnp.bfloat16
RIGHT = [(i, (i + 1) % 8) for i in range(8)]
LEFT = [(i, (i + 7) % 8) for i in range(8)]
SWAP = [(0, 1), (1, 0)]
BOTH = [(0, 3), (1, 2), (2, 1), (3, 0)]
FAR = [(0, 2), (1, 3), (2, 0), (3, 1)]
NEAR = [(0, 1), (1, 0), (2, 3), (3, 2)]


VMEM = pl.BlockSpec(memory_space=pltpu.VMEM)
SMEM = pl.BlockSpec(memory_space=pltpu.SMEM)
ROOM = pltpu.CompilerParams(vmem_limit_bytes=16 << 20)


def slopes_of(own, from_core, from_x, cotangent):
    tokens, width = own.shape

    def kernel(own_ref, core_ref, x_ref, cot_ref, out_ref):
        for h in range(width // HEAD):
            at = slice(h * HEAD, (h + 1) * HEAD)
            heads = own_ref[:, at] + core_ref[0, :, at].astype(F32) + x_ref[:, at].astype(F32)
            upstream = cot_ref[:, at].astype(F32)
            inverse = lax.rsqrt(jnp.mean(heads * heads, axis=-1, keepdims=True) + 1e-06)
            normed = heads * inverse
            along = jnp.mean(upstream * normed, axis=-1, keepdims=True)
            out_ref[:, at] = ((upstream - normed * along) * inverse).astype(BF16)

    return pl.pallas_call(
        kernel,
        in_specs=[VMEM] * 4,
        out_specs=VMEM,
        out_shape=jax.ShapeDtypeStruct((tokens, width), BF16),
        compiler_params=ROOM,
    )(own, from_core, from_x, cotangent)


def project(pieces, found):
    tokens, rows = pieces[0].shape[1:]
    width = found[0][1].shape[-1]

    def kernel(*refs):
        held, weights, total, blocks = refs[:4], refs[4 : 4 + len(found)], refs[4 + len(found)], refs[5 + len(found) :]
        for d in range(8):
            for k in range(4):
                blocks[d][k * tokens : (k + 1) * tokens, :] = held[k][d]
        for i, ((d, _), weight) in enumerate(zip(found, weights)):
            term = jnp.dot(blocks[d % 8][...], weight[...], preferred_element_type=F32)
            if i:
                total[...] += term
            else:
                total[...] = term

    total, *blocks = pl.pallas_call(
        kernel,
        in_specs=[VMEM] * (4 + len(found)),
        out_specs=[VMEM] * 9,
        out_shape=[jax.ShapeDtypeStruct((4 * tokens, width), F32)]
        + [jax.ShapeDtypeStruct((4 * tokens, rows), BF16)] * 8,
        compiler_params=ROOM,
    )(*pieces, *(block for _, block in found))
    return total, blocks


def complete(total, block, ends):
    tokens, width = total.shape[0] // 4, total.shape[1] // CUTS
    half = ends[0].shape[0]

    def kernel(total_ref, block_ref, up_ref, down_ref, *outs):
        for i in range(CUTS):
            at = slice(i * width, (i + 1) * width)
            sums = (
                total_ref[:, at]
                + jnp.dot(block_ref[:, :half], up_ref[:, at], preferred_element_type=F32)
                + jnp.dot(block_ref[:, half:], down_ref[:, at], preferred_element_type=F32)
            )
            own, over_x, crossing = outs[3 * i : 3 * i + 3]
            own[...] = sums[:tokens]
            over_x[...] = sums[tokens : 2 * tokens]
            crossing[0] = sums[2 * tokens : 3 * tokens].astype(BF16)
            crossing[1] = sums[3 * tokens :].astype(BF16)

    outs = pl.pallas_call(
        kernel,
        in_specs=[VMEM] * 4,
        out_specs=[VMEM] * (3 * CUTS),
        out_shape=[
            jax.ShapeDtypeStruct((tokens, width), F32),
            jax.ShapeDtypeStruct((tokens, width), F32),
            jax.ShapeDtypeStruct((2, tokens, width), BF16),
        ]
        * CUTS,
        compiler_params=ROOM,
    )(total, block, *ends)
    return [outs[3 * i : 3 * i + 3] for i in range(CUTS)]


def split_columns(rows, mine, z):
    tokens, width = rows.shape[0], rows.shape[1] // 32
    holds = ((2, 0, 8), (3, 0, 8), (1, 0, 8), (0, 0, 8))

    def kernel(mine_ref, z_ref, rows_ref, *refs):
        copies = []
        for (k, begin, count), out in zip(holds, refs):
            member = mine_ref[0] ^ k
            for i in range(count):
                at = lax.rem(z_ref[0] + begin + i, 8)
                start = pl.multiple_of((4 * at + member) * width, width)
                copies.append(
                    pltpu.make_async_copy(
                        rows_ref.at[:, pl.ds(start, width)], out.at[i], refs[-1].at[k, begin + i]
                    )
                )
                copies[-1].start()
        for copy in copies:
            copy.wait()

    over_x, over_both, core, own = pl.pallas_call(
        kernel,
        in_specs=[SMEM, SMEM, pl.BlockSpec(memory_space=pl.ANY)],
        out_specs=[VMEM] * len(holds),
        out_shape=[jax.ShapeDtypeStruct((count, tokens, width), rows.dtype) for _, _, count in holds],
        scratch_shapes=[pltpu.SemaphoreType.DMA((4, 8))],
        compiler_params=pltpu.CompilerParams(vmem_limit_bytes=16 << 20),
    )(mine, z, rows)
    return own, core, over_x, over_both


def tie(value, *others):
    return lax.optimization_barrier((value, *others))[0]


def step(pair, *others):
    pair = lax.optimization_barrier((*pair, *others))
    return lax.ppermute(pair[0], "z", RIGHT), lax.ppermute(pair[1], "z", LEFT)


def ends(pair):
    half = pair[0].shape[0] // 2
    return pair[0][:half], pair[1][half:]


def plus(part, arrived):
    return (part + arrived.astype(F32)).astype(BF16)


def beside(part_of, arrived):
    up, down = arrived
    half = up.shape[0]
    ahead, behind = part_of(3), part_of(-3)
    return (
        jnp.concatenate([plus(ahead[:half], up), ahead[half:].astype(BF16)]),
        jnp.concatenate([behind[:half].astype(BF16), plus(behind[half:], down)]),
    )


def onward(part_of, arrived, d):
    return plus(part_of(d), arrived[0]), plus(part_of(-d), arrived[1])


def home(part_of, arrived):
    return part_of(0) + arrived[0].astype(F32) + arrived[1].astype(F32)


def body(activations, inner_weight, out_cotangent, local_fragment, outer_base, outer_momentum):
    weight, fragment = inner_weight[0], local_fragment[0]
    y = lax.axis_index("y")
    mine = lax.axis_index("xh") * 2 + lax.axis_index("c")
    bits = [(y & 2) == 2, (y & 1) == 1, lax.axis_index("xl") == 1]
    weight, activations, fragment, z, mine, *bits = lax.optimization_barrier(
        (weight, activations, fragment, lax.axis_index("z").reshape(1), mine.reshape(1), *bits)
    )

    own_rows, own_columns = outer_base.shape
    stages = ((1, "y", FAR), (2, "y", NEAR), (0, "xl", SWAP))

    def halve(total, stage, *others):
        at, axis, moves = stages[stage]
        low, high = jnp.split(total, 2, axis=at)
        sent = tie(jnp.where(bits[stage], low, high), *others)
        return jnp.where(bits[stage], high, low).astype(F32) + lax.ppermute(sent, axis, moves).astype(F32)

    def double(rows, stage, *others):
        at, axis, moves = stages[stage]
        other = lax.ppermute(tie(rows, *others), axis, moves)
        low, high = jnp.where(bits[stage], other, rows), jnp.where(bits[stage], rows, other)
        return jnp.concatenate([low, high], axis=at)

    a1 = step((weight, weight))
    own, core, over_x, over_both = split_columns(activations, mine, z)
    from_x = lax.ppermute(over_x, "xh", SWAP)
    from_core = lax.ppermute(core, "c", SWAP)
    a2 = step(a1)
    from_both = lax.ppermute(tie(over_both, from_x), ("xh", "c"), BOTH)
    total = halve(fragment.reshape(2, 2, 2, own_rows, own_columns), 0, *a1)
    a3 = step(a2, from_core, total)
    total = halve(total, 1, *a2)
    a4 = step(ends(a3), total)

    found = [(0, weight)]
    for d, pair in enumerate((a1, a2, a3), 1):
        found += [(-d, pair[0]), (d, pair[1])]
    sums, blocks = project((own, from_x, from_core, from_both), found)
    total = halve(total, 2, sums)
    partial = complete(sums, blocks[4], a4)
    width = weight.shape[1] // CUTS

    def part_with(slopes):
        return lambda d: lax.dot_general(
            blocks[d % 8], slopes, (((0,), (0,)), ((), ())), preferred_element_type=F32
        )

    def slopes_from(own, from_core, from_x, cut):
        cotangent = out_cotangent[:, cut * width : (cut + 1) * width]
        mine = slopes_of(own, from_core, from_x, cotangent)
        pair = jnp.stack([mine, lax.ppermute(mine, "xh", SWAP)])
        return jnp.concatenate([pair, lax.ppermute(pair, "c", SWAP)]).reshape(-1, width)

    crossed = [lax.ppermute(crossing, "c", SWAP) for _, _, crossing in partial]
    arrived = [
        lax.ppermute(plus(over_x, from_core[1]), "xh", SWAP)
        for (_, over_x, _), from_core in zip(partial, crossed)
    ]
    slopes = slopes_from(partial[0][0], crossed[0], arrived[0], 0)
    first = part_with(slopes)

    far = first(4).astype(BF16)
    t1 = step(ends((far, far)), arrived[1])
    slopes = slopes_from(partial[1][0], crossed[1], arrived[1], 1)
    second = part_with(slopes)
    delta = outer_base - total.reshape(own_rows, own_columns) / 8
    new_momentum = 0.9 * outer_momentum + delta
    new_base = outer_base - 0.7 * (delta + 0.9 * new_momentum)
    half_base = double(new_base.astype(BF16).reshape(1, 1, 1, own_rows, own_columns), 2)
    t2 = step(beside(first, t1), half_base)
    half_base = double(half_base, 1, *t1)
    far = second(4).astype(BF16)
    t3 = step(onward(first, t2, 2), slopes, half_base)
    u1 = step(ends((far, far)), *t2)
    half_base = double(half_base, 0, *t2)
    t4 = step(onward(first, t3, 1), *u1, half_base)
    u2 = step(beside(second, u1), *t3)
    u3 = step(onward(second, u2, 2), *t4)
    u4 = step(onward(second, u3, 1))
    grad = jnp.concatenate([home(first, t4), home(second, u4)], axis=1)
    half_base = half_base.reshape(fragment.shape)
    merged = (0.5 * half_base.astype(F32) + 0.5 * fragment.astype(F32)).astype(BF16)
    return grad[None], new_base, new_momentum, merged[None]


def solution(mesh):
    axes = ("xl", "y", "z", "xh", "c")
    mesh = Mesh(mesh.devices.reshape(2, 4, 8, 2, 2), axes)
    replica, fsdp = ("xl", "y"), ("z", "xh", "c")
    placed = (
        P(axes, None),
        P(replica, fsdp, None),
        P(axes, None),
        P(replica, None, fsdp),
        P(replica, fsdp),
        P(replica, fsdp),
    )
    return jax.shard_map(
        body,
        mesh=mesh,
        in_specs=placed,
        out_specs=(
            P(replica, fsdp, None),
            P(replica, fsdp),
            P(replica, fsdp),
            P(replica, None, fsdp),
        ),
        check_vma=False,
    )
```

```python
import jax
import jax.numpy as jnp
from jax import lax
from jax.experimental import pallas as pl
from jax.experimental.pallas import tpu as pltpu
from jax.sharding import Mesh, PartitionSpec as P

HEAD = 128
CUT = 512
F32, BF16 = jnp.float32, jnp.bfloat16
RIGHT = [(i, (i + 1) % 8) for i in range(8)]
LEFT = [(i, (i + 7) % 8) for i in range(8)]
SWAP = [(0, 1), (1, 0)]
BOTH = [(0, 3), (1, 2), (2, 1), (3, 0)]
FAR = [(0, 2), (1, 3), (2, 0), (3, 1)]
NEAR = [(0, 1), (1, 0), (2, 3), (3, 2)]


VMEM = pl.BlockSpec(memory_space=pltpu.VMEM)
SMEM = pl.BlockSpec(memory_space=pltpu.SMEM)
ROOM = pltpu.CompilerParams(vmem_limit_bytes=16 << 20)


def slopes_of(own, from_core, from_x, cotangent):
    tokens, width = own.shape

    def kernel(own_ref, core_ref, x_ref, cot_ref, out_ref):
        for h in range(width // HEAD):
            at = slice(h * HEAD, (h + 1) * HEAD)
            heads = own_ref[:, at] + core_ref[0, :, at].astype(F32) + x_ref[:, at].astype(F32)
            upstream = cot_ref[:, at].astype(F32)
            inverse = lax.rsqrt(jnp.mean(heads * heads, axis=-1, keepdims=True) + 1e-06)
            normed = heads * inverse
            along = jnp.mean(upstream * normed, axis=-1, keepdims=True)
            out_ref[:, at] = ((upstream - normed * along) * inverse).astype(BF16)

    return pl.pallas_call(
        kernel,
        in_specs=[VMEM] * 4,
        out_specs=VMEM,
        out_shape=jax.ShapeDtypeStruct((tokens, width), BF16),
        compiler_params=ROOM,
    )(own, from_core, from_x, cotangent)


def project(pieces, blocks, found):
    tokens, rows = pieces[0].shape[1:]
    width = found[0][1].shape[-1]
    taken = blocks or pieces

    def kernel(*refs):
        held, weights, total = refs[: len(taken)], refs[len(taken) : len(taken) + len(found)], refs[len(taken) + len(found)]
        made = held if blocks else refs[len(taken) + len(found) + 1 :]
        if not blocks:
            for d in range(8):
                for k in range(4):
                    made[d][k * tokens : (k + 1) * tokens, :] = held[k][d]
        for i, ((d, _), weight) in enumerate(zip(found, weights)):
            term = jnp.dot(made[d % 8][...], weight[...], preferred_element_type=F32)
            if i:
                total[...] += term
            else:
                total[...] = term

    shapes = [jax.ShapeDtypeStruct((4 * tokens, width), F32)]
    if not blocks:
        shapes += [jax.ShapeDtypeStruct((4 * tokens, rows), BF16)] * 8
    total, *made = pl.pallas_call(
        kernel,
        in_specs=[VMEM] * (len(taken) + len(found)),
        out_specs=[VMEM] * len(shapes),
        out_shape=shapes,
        compiler_params=ROOM,
    )(*taken, *(block for _, block in found))
    return total, blocks or made


def complete(total, block, ends):
    tokens, width = total.shape[0] // 4, total.shape[1]
    half = ends[0].shape[0]

    def kernel(total_ref, block_ref, up_ref, down_ref, own, over_x, crossing):
        sums = (
            total_ref[...]
            + jnp.dot(block_ref[:, :half], up_ref[...], preferred_element_type=F32)
            + jnp.dot(block_ref[:, half:], down_ref[...], preferred_element_type=F32)
        )
        own[...] = sums[:tokens]
        over_x[...] = sums[tokens : 2 * tokens]
        crossing[0] = sums[2 * tokens : 3 * tokens].astype(BF16)
        crossing[1] = sums[3 * tokens :].astype(BF16)

    return pl.pallas_call(
        kernel,
        in_specs=[VMEM] * 4,
        out_specs=[VMEM] * 3,
        out_shape=[
            jax.ShapeDtypeStruct((tokens, width), F32),
            jax.ShapeDtypeStruct((tokens, width), F32),
            jax.ShapeDtypeStruct((2, tokens, width), BF16),
        ],
        compiler_params=ROOM,
    )(total, block, *ends)


def cut_columns(weight):
    rows, width = weight.shape
    edges = ((0, CUT), (CUT, width))

    def kernel(weight_ref, *refs):
        copies = [
            pltpu.make_async_copy(weight_ref.at[:, pl.ds(a, b - a)], out, refs[2].at[i])
            for i, ((a, b), out) in enumerate(zip(edges, refs))
        ]
        for copy in copies:
            copy.start()
        for copy in copies:
            copy.wait()

    return pl.pallas_call(
        kernel,
        in_specs=[pl.BlockSpec(memory_space=pl.ANY)],
        out_specs=[VMEM] * 2,
        out_shape=[jax.ShapeDtypeStruct((rows, b - a), weight.dtype) for a, b in edges],
        scratch_shapes=[pltpu.SemaphoreType.DMA((2,))],
        compiler_params=ROOM,
    )(weight)


def split_columns(rows, mine, z):
    tokens, width = rows.shape[0], rows.shape[1] // 32
    holds = ((2, 0, 8), (3, 0, 8), (1, 0, 8), (0, 0, 8))

    def kernel(mine_ref, z_ref, rows_ref, *refs):
        copies = []
        for (k, begin, count), out in zip(holds, refs):
            member = mine_ref[0] ^ k
            for i in range(count):
                at = lax.rem(z_ref[0] + begin + i, 8)
                start = pl.multiple_of((4 * at + member) * width, width)
                copies.append(
                    pltpu.make_async_copy(
                        rows_ref.at[:, pl.ds(start, width)], out.at[i], refs[-1].at[k, begin + i]
                    )
                )
                copies[-1].start()
        for copy in copies:
            copy.wait()

    over_x, over_both, core, own = pl.pallas_call(
        kernel,
        in_specs=[SMEM, SMEM, pl.BlockSpec(memory_space=pl.ANY)],
        out_specs=[VMEM] * len(holds),
        out_shape=[jax.ShapeDtypeStruct((count, tokens, width), rows.dtype) for _, _, count in holds],
        scratch_shapes=[pltpu.SemaphoreType.DMA((4, 8))],
        compiler_params=pltpu.CompilerParams(vmem_limit_bytes=16 << 20),
    )(mine, z, rows)
    return own, core, over_x, over_both


def tie(value, *others):
    return lax.optimization_barrier((value, *others))[0]


def step(pair, *others):
    pair = lax.optimization_barrier((*pair, *others))
    return lax.ppermute(pair[0], "z", RIGHT), lax.ppermute(pair[1], "z", LEFT)


def ends(pair):
    half = pair[0].shape[0] // 2
    return pair[0][:half], pair[1][half:]


def plus(part, arrived):
    return (part + arrived.astype(F32)).astype(BF16)


def beside(part_of, arrived):
    up, down = arrived
    half = up.shape[0]
    ahead, behind = part_of(3), part_of(-3)
    return (
        jnp.concatenate([plus(ahead[:half], up), ahead[half:].astype(BF16)]),
        jnp.concatenate([behind[:half].astype(BF16), plus(behind[half:], down)]),
    )


def onward(part_of, arrived, d):
    return plus(part_of(d), arrived[0]), plus(part_of(-d), arrived[1])


def home(part_of, arrived):
    return part_of(0) + arrived[0].astype(F32) + arrived[1].astype(F32)


def body(activations, inner_weight, out_cotangent, local_fragment, outer_base, outer_momentum):
    weight, fragment = inner_weight[0], local_fragment[0]
    y = lax.axis_index("y")
    mine = lax.axis_index("xh") * 2 + lax.axis_index("c")
    bits = [(y & 2) == 2, (y & 1) == 1, lax.axis_index("xl") == 1]
    weight, activations, fragment, z, mine, *bits = lax.optimization_barrier(
        (weight, activations, fragment, lax.axis_index("z").reshape(1), mine.reshape(1), *bits)
    )

    own_rows, own_columns = outer_base.shape
    stages = ((1, "y", FAR), (2, "y", NEAR), (0, "xl", SWAP))

    def halve(total, stage, *others):
        at, axis, moves = stages[stage]
        low, high = jnp.split(total, 2, axis=at)
        sent = tie(jnp.where(bits[stage], low, high), *others)
        return jnp.where(bits[stage], high, low).astype(F32) + lax.ppermute(sent, axis, moves).astype(F32)

    def double(rows, stage, *others):
        at, axis, moves = stages[stage]
        other = lax.ppermute(tie(rows, *others), axis, moves)
        low, high = jnp.where(bits[stage], other, rows), jnp.where(bits[stage], rows, other)
        return jnp.concatenate([low, high], axis=at)

    def near(shard, one, two, three):
        return [(0, shard)] + [(s * d, p) for d, pair in enumerate((one, two, three), 1) for s, p in zip((-1, 1), pair)]

    def part_with(slopes):
        return lambda d: lax.dot_general(
            blocks[d % 8], slopes, (((0,), (0,)), ((), ())), preferred_element_type=F32
        )

    def slopes_from(own, from_core, from_x, cotangent):
        mine = slopes_of(own, from_core, from_x, cotangent)
        pair = jnp.stack([mine, lax.ppermute(mine, "xh", SWAP)])
        return jnp.concatenate([pair, lax.ppermute(pair, "c", SWAP)]).reshape(-1, mine.shape[1])

    shards = cut_columns(weight)
    a1 = step((shards[0], shards[0]))
    own, core, over_x, over_both = split_columns(tie(activations, shards[0]), mine, z)
    from_x = lax.ppermute(over_x, "xh", SWAP)
    from_core = lax.ppermute(core, "c", SWAP)
    b1 = step((shards[1], shards[1]))
    a2, b2 = step(a1), step(b1)
    from_both = lax.ppermute(tie(over_both, from_x), ("xh", "c"), BOTH)
    total = halve(fragment.reshape(2, 2, 2, own_rows, own_columns), 0, *a1)
    a3, b3 = step(a2, from_core, total), step(b2)
    total = halve(total, 1, *a2)
    a4, b4 = step(ends(a3), total), step(ends(b3))

    pieces = (own, from_x, from_core, from_both)
    sums, blocks = project(pieces, None, near(shards[0], a1, a2, a3))
    partial = [complete(sums, blocks[4], a4)]
    sums, _ = project(pieces, blocks, near(shards[1], b1, b2, b3))
    partial += [complete(sums, blocks[4], b4)]
    crossed = [lax.ppermute(crossing, "c", SWAP) for _, _, crossing in partial]
    arrived = [
        lax.ppermute(plus(over_x, from_core[1]), "xh", SWAP)
        for (_, over_x, _), from_core in zip(partial, crossed)
    ]
    slopes = slopes_from(partial[0][0], crossed[0], arrived[0], out_cotangent[:, :CUT])
    first = part_with(slopes)

    far = first(4).astype(BF16)
    t1 = step(ends((far, far)))
    total = halve(total, 2, slopes)
    slopes = slopes_from(partial[1][0], crossed[1], arrived[1], out_cotangent[:, CUT:])
    second = part_with(slopes)
    far = second(4).astype(BF16)
    u1 = step(ends((far, far)))
    delta = outer_base - total.reshape(own_rows, own_columns) / 8
    new_momentum = 0.9 * outer_momentum + delta
    new_base = outer_base - 0.7 * (delta + 0.9 * new_momentum)
    t2 = step(beside(first, t1))
    half_base = double(new_base.astype(BF16).reshape(1, 1, 1, own_rows, own_columns), 2, *t1)
    u2 = step(beside(second, u1), new_base)
    t3 = step(onward(first, t2, 2), half_base)
    half_base = double(half_base, 1, *t2)
    u3 = step(onward(second, u2, 2))
    t4 = step(onward(first, t3, 1), half_base)
    half_base = double(half_base, 0, *t3)
    u4 = step(onward(second, u3, 1))
    grad = jnp.concatenate([home(first, t4), home(second, u4)], axis=1)
    half_base = half_base.reshape(fragment.shape)
    merged = (0.5 * half_base.astype(F32) + 0.5 * fragment.astype(F32)).astype(BF16)
    return grad[None], new_base, new_momentum, merged[None]


def solution(mesh):
    axes = ("xl", "y", "z", "xh", "c")
    mesh = Mesh(mesh.devices.reshape(2, 4, 8, 2, 2), axes)
    replica, fsdp = ("xl", "y"), ("z", "xh", "c")
    placed = (
        P(axes, None),
        P(replica, fsdp, None),
        P(axes, None),
        P(replica, None, fsdp),
        P(replica, fsdp),
        P(replica, fsdp),
    )
    return jax.shard_map(
        body,
        mesh=mesh,
        in_specs=placed,
        out_specs=(
            P(replica, fsdp, None),
            P(replica, fsdp),
            P(replica, fsdp),
            P(replica, None, fsdp),
        ),
        check_vma=False,
    )
```

```python
import jax
import jax.numpy as jnp
from jax import lax
from jax.experimental import pallas as pl
from jax.experimental.pallas import tpu as pltpu
from jax.sharding import Mesh, PartitionSpec as P

HEAD = 128
CUT = 512
F32, BF16 = jnp.float32, jnp.bfloat16
RIGHT = [(i, (i + 1) % 8) for i in range(8)]
LEFT = [(i, (i + 7) % 8) for i in range(8)]
SWAP = [(0, 1), (1, 0)]
BOTH = [(0, 3), (1, 2), (2, 1), (3, 0)]
FAR = [(0, 2), (1, 3), (2, 0), (3, 1)]
NEAR = [(0, 1), (1, 0), (2, 3), (3, 2)]


VMEM = pl.BlockSpec(memory_space=pltpu.VMEM)
SMEM = pl.BlockSpec(memory_space=pltpu.SMEM)
ROOM = pltpu.CompilerParams(vmem_limit_bytes=16 << 20)


def slopes_of(own, from_core, from_x, cotangent):
    tokens, width = own.shape

    def kernel(own_ref, core_ref, x_ref, cot_ref, out_ref):
        for h in range(width // HEAD):
            at = slice(h * HEAD, (h + 1) * HEAD)
            heads = own_ref[:, at] + core_ref[0, :, at].astype(F32) + x_ref[:, at].astype(F32)
            upstream = cot_ref[:, at].astype(F32)
            inverse = lax.rsqrt(jnp.mean(heads * heads, axis=-1, keepdims=True) + 1e-06)
            normed = heads * inverse
            along = jnp.mean(upstream * normed, axis=-1, keepdims=True)
            out_ref[:, at] = ((upstream - normed * along) * inverse).astype(BF16)

    return pl.pallas_call(
        kernel,
        in_specs=[VMEM] * 4,
        out_specs=VMEM,
        out_shape=jax.ShapeDtypeStruct((tokens, width), BF16),
        compiler_params=ROOM,
    )(own, from_core, from_x, cotangent)


def project(pieces, blocks, found):
    tokens, rows = pieces[0].shape[1:]
    width = found[0][1].shape[-1]
    taken = blocks or pieces

    def kernel(*refs):
        held, weights, total = refs[: len(taken)], refs[len(taken) : len(taken) + len(found)], refs[len(taken) + len(found)]
        made = held if blocks else refs[len(taken) + len(found) + 1 :]
        if not blocks:
            for d in range(8):
                for k in range(4):
                    made[d][k * tokens : (k + 1) * tokens, :] = held[k][d]
        for i, ((d, _), weight) in enumerate(zip(found, weights)):
            term = jnp.dot(made[d % 8][...], weight[...], preferred_element_type=F32)
            if i:
                total[...] += term
            else:
                total[...] = term

    shapes = [jax.ShapeDtypeStruct((4 * tokens, width), F32)]
    if not blocks:
        shapes += [jax.ShapeDtypeStruct((4 * tokens, rows), BF16)] * 8
    total, *made = pl.pallas_call(
        kernel,
        in_specs=[VMEM] * (len(taken) + len(found)),
        out_specs=[VMEM] * len(shapes),
        out_shape=shapes,
        compiler_params=ROOM,
    )(*taken, *(block for _, block in found))
    return total, blocks or made


def complete(total, block, ends):
    tokens, width = total.shape[0] // 4, total.shape[1]
    half = ends[0].shape[0]

    def kernel(total_ref, block_ref, up_ref, down_ref, own, over_x, crossing):
        sums = (
            total_ref[...]
            + jnp.dot(block_ref[:, :half], up_ref[...], preferred_element_type=F32)
            + jnp.dot(block_ref[:, half:], down_ref[...], preferred_element_type=F32)
        )
        own[...] = sums[:tokens]
        over_x[...] = sums[tokens : 2 * tokens]
        crossing[0] = sums[2 * tokens : 3 * tokens].astype(BF16)
        crossing[1] = sums[3 * tokens :].astype(BF16)

    return pl.pallas_call(
        kernel,
        in_specs=[VMEM] * 4,
        out_specs=[VMEM] * 3,
        out_shape=[
            jax.ShapeDtypeStruct((tokens, width), F32),
            jax.ShapeDtypeStruct((tokens, width), F32),
            jax.ShapeDtypeStruct((2, tokens, width), BF16),
        ],
        compiler_params=ROOM,
    )(total, block, *ends)


def cut_columns(weight):
    rows, width = weight.shape
    edges = ((0, CUT), (CUT, width))

    def kernel(weight_ref, *refs):
        copies = [
            pltpu.make_async_copy(weight_ref.at[:, pl.ds(a, b - a)], out, refs[2].at[i])
            for i, ((a, b), out) in enumerate(zip(edges, refs))
        ]
        for copy in copies:
            copy.start()
        for copy in copies:
            copy.wait()

    return pl.pallas_call(
        kernel,
        in_specs=[pl.BlockSpec(memory_space=pl.ANY)],
        out_specs=[VMEM] * 2,
        out_shape=[jax.ShapeDtypeStruct((rows, b - a), weight.dtype) for a, b in edges],
        scratch_shapes=[pltpu.SemaphoreType.DMA((2,))],
        compiler_params=ROOM,
    )(weight)


def split_columns(rows, mine, z):
    tokens, width = rows.shape[0], rows.shape[1] // 32
    holds = ((2, 0, 8), (3, 0, 8), (1, 0, 8), (0, 0, 8))

    def kernel(mine_ref, z_ref, rows_ref, *refs):
        copies = []
        for (k, begin, count), out in zip(holds, refs):
            member = mine_ref[0] ^ k
            for i in range(count):
                at = lax.rem(z_ref[0] + begin + i, 8)
                start = pl.multiple_of((4 * at + member) * width, width)
                copies.append(
                    pltpu.make_async_copy(
                        rows_ref.at[:, pl.ds(start, width)], out.at[i], refs[-1].at[k, begin + i]
                    )
                )
                copies[-1].start()
        for copy in copies:
            copy.wait()

    over_x, over_both, core, own = pl.pallas_call(
        kernel,
        in_specs=[SMEM, SMEM, pl.BlockSpec(memory_space=pl.ANY)],
        out_specs=[VMEM] * len(holds),
        out_shape=[jax.ShapeDtypeStruct((count, tokens, width), rows.dtype) for _, _, count in holds],
        scratch_shapes=[pltpu.SemaphoreType.DMA((4, 8))],
        compiler_params=pltpu.CompilerParams(vmem_limit_bytes=16 << 20),
    )(mine, z, rows)
    return own, core, over_x, over_both


def tie(value, *others):
    return lax.optimization_barrier((value, *others))[0]


def step(pair, *others):
    pair = lax.optimization_barrier((*pair, *others))
    return lax.ppermute(pair[0], "z", RIGHT), lax.ppermute(pair[1], "z", LEFT)


def ends(pair):
    half = pair[0].shape[0] // 2
    return pair[0][:half], pair[1][half:]


def plus(part, arrived):
    return (part + arrived.astype(F32)).astype(BF16)


def beside(part_of, arrived):
    up, down = arrived
    half = up.shape[0]
    ahead, behind = part_of(3), part_of(-3)
    return (
        jnp.concatenate([plus(ahead[:half], up), ahead[half:].astype(BF16)]),
        jnp.concatenate([behind[:half].astype(BF16), plus(behind[half:], down)]),
    )


def onward(part_of, arrived, d):
    return plus(part_of(d), arrived[0]), plus(part_of(-d), arrived[1])


def side_by_side(*cuts):
    rows = cuts[0][0].shape[0]
    widths = [part.shape[1] for part, _, _ in cuts]
    edges = [sum(widths[:i]) for i in range(len(cuts) + 1)]

    def kernel(*refs):
        for i in range(len(cuts)):
            part, up, down = refs[3 * i : 3 * i + 3]
            refs[-1][:, edges[i] : edges[i + 1]] = part[...] + up[...].astype(F32) + down[...].astype(F32)

    return pl.pallas_call(
        kernel,
        in_specs=[VMEM] * (3 * len(cuts)),
        out_specs=VMEM,
        out_shape=jax.ShapeDtypeStruct((rows, edges[-1]), F32),
        compiler_params=ROOM,
    )(*(array for cut in cuts for array in cut))


def body(activations, inner_weight, out_cotangent, local_fragment, outer_base, outer_momentum):
    weight, fragment = inner_weight[0], local_fragment[0]
    y = lax.axis_index("y")
    mine = lax.axis_index("xh") * 2 + lax.axis_index("c")
    bits = [(y & 2) == 2, (y & 1) == 1, lax.axis_index("xl") == 1]
    weight, activations, fragment, z, mine, *bits = lax.optimization_barrier(
        (weight, activations, fragment, lax.axis_index("z").reshape(1), mine.reshape(1), *bits)
    )

    own_rows, own_columns = outer_base.shape
    stages = ((1, "y", FAR), (2, "y", NEAR), (0, "xl", SWAP))

    def halve(total, stage, *others):
        at, axis, moves = stages[stage]
        low, high = jnp.split(total, 2, axis=at)
        sent = tie(jnp.where(bits[stage], low, high), *others)
        return jnp.where(bits[stage], high, low).astype(F32) + lax.ppermute(sent, axis, moves).astype(F32)

    def double(rows, stage, *others):
        at, axis, moves = stages[stage]
        other = lax.ppermute(tie(rows, *others), axis, moves)
        low, high = jnp.where(bits[stage], other, rows), jnp.where(bits[stage], rows, other)
        return jnp.concatenate([low, high], axis=at)

    def near(shard, one, two, three):
        return [(0, shard)] + [(s * d, p) for d, pair in enumerate((one, two, three), 1) for s, p in zip((-1, 1), pair)]

    def part_with(slopes):
        return lambda d: lax.dot_general(
            blocks[d % 8], slopes, (((0,), (0,)), ((), ())), preferred_element_type=F32
        )

    def slopes_from(own, from_core, from_x, cotangent):
        mine = slopes_of(own, from_core, from_x, cotangent)
        from_both = lax.ppermute(mine, ("xh", "c"), BOTH)
        return jnp.concatenate([mine, lax.ppermute(mine, "xh", SWAP), lax.ppermute(mine, "c", SWAP), from_both])

    shards = cut_columns(weight)
    a1 = step((shards[0], shards[0]))
    own, core, over_x, over_both = split_columns(tie(activations, shards[0]), mine, z)
    from_x = lax.ppermute(over_x, "xh", SWAP)
    from_core = lax.ppermute(core, "c", SWAP)
    b1 = step((shards[1], shards[1]))
    a2, b2 = step(a1), step(b1)
    from_both = lax.ppermute(tie(over_both, from_x), ("xh", "c"), BOTH)
    total = halve(fragment.reshape(2, 2, 2, own_rows, own_columns), 0, *a1)
    a3, b3 = step(a2, from_core, total), step(b2)
    total = halve(total, 1, *a2)
    a4, b4 = step(ends(a3), total), step(ends(b3))

    pieces = (own, from_x, from_core, from_both)
    sums, blocks = project(pieces, None, near(shards[0], a1, a2, a3))
    partial = [complete(sums, blocks[4], a4)]
    sums, _ = project(pieces, blocks, near(shards[1], b1, b2, b3))
    partial += [complete(sums, blocks[4], b4)]
    crossed = [lax.ppermute(crossing, "c", SWAP) for _, _, crossing in partial]
    arrived = [
        lax.ppermute(plus(over_x, from_core[1]), "xh", SWAP)
        for (_, over_x, _), from_core in zip(partial, crossed)
    ]
    slopes = slopes_from(partial[0][0], crossed[0], arrived[0], out_cotangent[:, :CUT])
    first = part_with(slopes)

    far = first(4).astype(BF16)
    t1 = step(ends((far, far)))
    total = halve(total, 2, *t1)
    slopes = slopes_from(partial[1][0], crossed[1], arrived[1], out_cotangent[:, CUT:])
    second = part_with(slopes)
    far = second(4).astype(BF16)
    u1 = step(ends((far, far)))
    delta = outer_base - total.reshape(own_rows, own_columns) / 8
    new_momentum = 0.9 * outer_momentum + delta
    new_base = outer_base - 0.7 * (delta + 0.9 * new_momentum)
    t2 = step(beside(first, t1))
    half_base = double(new_base.astype(BF16).reshape(1, 1, 1, own_rows, own_columns), 2, *t1)
    u2 = step(beside(second, u1), new_base)
    t3 = step(onward(first, t2, 2), half_base)
    half_base = double(half_base, 1, *t2)
    u3 = step(onward(second, u2, 2))
    t4 = step(onward(first, t3, 1), half_base)
    half_base = double(half_base, 0, *t3)
    u4 = step(onward(second, u3, 1))
    grad = side_by_side((first(0), *t4), (second(0), *u4))
    half_base = half_base.reshape(fragment.shape)
    merged = (0.5 * half_base.astype(F32) + 0.5 * fragment.astype(F32)).astype(BF16)
    return grad[None], new_base, new_momentum, merged[None]


def solution(mesh):
    axes = ("xl", "y", "z", "xh", "c")
    mesh = Mesh(mesh.devices.reshape(2, 4, 8, 2, 2), axes)
    replica, fsdp = ("xl", "y"), ("z", "xh", "c")
    placed = (
        P(axes, None),
        P(replica, fsdp, None),
        P(axes, None),
        P(replica, None, fsdp),
        P(replica, fsdp),
        P(replica, fsdp),
    )
    return jax.shard_map(
        body,
        mesh=mesh,
        in_specs=placed,
        out_specs=(
            P(replica, fsdp, None),
            P(replica, fsdp),
            P(replica, fsdp),
            P(replica, None, fsdp),
        ),
        check_vma=False,
    )
```

```python
import jax
import jax.numpy as jnp
from jax import lax
from jax.experimental import pallas as pl
from jax.experimental.pallas import tpu as pltpu
from jax.sharding import Mesh, PartitionSpec as P

HEAD = 128
CUT = 512
F32, BF16 = jnp.float32, jnp.bfloat16
RIGHT = [(i, (i + 1) % 8) for i in range(8)]
LEFT = [(i, (i + 7) % 8) for i in range(8)]
SWAP = [(0, 1), (1, 0)]
BOTH = [(0, 3), (1, 2), (2, 1), (3, 0)]
FAR = [(0, 2), (1, 3), (2, 0), (3, 1)]
NEAR = [(0, 1), (1, 0), (2, 3), (3, 2)]


VMEM = pl.BlockSpec(memory_space=pltpu.VMEM)
SMEM = pl.BlockSpec(memory_space=pltpu.SMEM)
ROOM = pltpu.CompilerParams(vmem_limit_bytes=16 << 20)


def slopes_of(own, from_core, from_x, cotangent):
    tokens, width = own.shape

    def kernel(own_ref, core_ref, x_ref, cot_ref, out_ref):
        for h in range(width // HEAD):
            at = slice(h * HEAD, (h + 1) * HEAD)
            heads = own_ref[:, at] + core_ref[0, :, at].astype(F32) + x_ref[:, at].astype(F32)
            upstream = cot_ref[:, at].astype(F32)
            inverse = lax.rsqrt(jnp.mean(heads * heads, axis=-1, keepdims=True) + 1e-06)
            normed = heads * inverse
            along = jnp.mean(upstream * normed, axis=-1, keepdims=True)
            out_ref[:, at] = ((upstream - normed * along) * inverse).astype(BF16)

    return pl.pallas_call(
        kernel,
        in_specs=[VMEM] * 4,
        out_specs=VMEM,
        out_shape=jax.ShapeDtypeStruct((tokens, width), BF16),
        compiler_params=ROOM,
    )(own, from_core, from_x, cotangent)


def project(pieces, founds):
    tokens, rows = pieces[0].shape[1:]
    arrays = [block for found in founds for _, block in found]

    def kernel(*refs):
        held, weights, outs = refs[:4], refs[4 : 4 + len(arrays)], refs[4 + len(arrays) :]
        totals, blocks = outs[: len(founds)], outs[len(founds) :]
        for d in range(8):
            for k in range(4):
                blocks[d][k * tokens : (k + 1) * tokens, :] = held[k][d]
        weights = iter(weights)
        for found, total in zip(founds, totals):
            for i, (d, _) in enumerate(found):
                term = jnp.dot(blocks[d % 8][...], next(weights)[...], preferred_element_type=F32)
                if i:
                    total[...] += term
                else:
                    total[...] = term

    outs = pl.pallas_call(
        kernel,
        in_specs=[VMEM] * (4 + len(arrays)),
        out_specs=[VMEM] * (len(founds) + 8),
        out_shape=[jax.ShapeDtypeStruct((4 * tokens, found[0][1].shape[1]), F32) for found in founds]
        + [jax.ShapeDtypeStruct((4 * tokens, rows), BF16)] * 8,
        compiler_params=ROOM,
    )(*pieces, *arrays)
    return outs[: len(founds)], outs[len(founds) :]


def complete(totals, block, lasts):
    tokens = totals[0].shape[0] // 4
    half = lasts[0][0].shape[0]

    def kernel(block_ref, *refs):
        given, outs = refs[: 3 * len(totals)], refs[3 * len(totals) :]
        for i in range(len(totals)):
            total, up, down = given[3 * i : 3 * i + 3]
            own, over_x, crossing = outs[3 * i : 3 * i + 3]
            sums = (
                total[...]
                + jnp.dot(block_ref[:, :half], up[...], preferred_element_type=F32)
                + jnp.dot(block_ref[:, half:], down[...], preferred_element_type=F32)
            )
            own[...] = sums[:tokens]
            over_x[...] = sums[tokens : 2 * tokens]
            crossing[0] = sums[2 * tokens : 3 * tokens].astype(BF16)
            crossing[1] = sums[3 * tokens :].astype(BF16)

    shapes = []
    for total in totals:
        width = total.shape[1]
        shapes += [jax.ShapeDtypeStruct((tokens, width), F32)] * 2 + [jax.ShapeDtypeStruct((2, tokens, width), BF16)]
    outs = pl.pallas_call(
        kernel,
        in_specs=[VMEM] * (1 + 3 * len(totals)),
        out_specs=[VMEM] * len(shapes),
        out_shape=shapes,
        compiler_params=ROOM,
    )(block, *(array for total, pair in zip(totals, lasts) for array in (total, *pair)))
    return [outs[3 * i : 3 * i + 3] for i in range(len(totals))]


def cut_columns(weight):
    rows, width = weight.shape
    edges = ((0, CUT), (CUT, width))

    def kernel(weight_ref, *refs):
        copies = [
            pltpu.make_async_copy(weight_ref.at[:, pl.ds(a, b - a)], out, refs[2].at[i])
            for i, ((a, b), out) in enumerate(zip(edges, refs))
        ]
        for copy in copies:
            copy.start()
        for copy in copies:
            copy.wait()

    return pl.pallas_call(
        kernel,
        in_specs=[pl.BlockSpec(memory_space=pl.ANY)],
        out_specs=[VMEM] * 2,
        out_shape=[jax.ShapeDtypeStruct((rows, b - a), weight.dtype) for a, b in edges],
        scratch_shapes=[pltpu.SemaphoreType.DMA((2,))],
        compiler_params=ROOM,
    )(weight)


def split_columns(rows, mine, z):
    tokens, width = rows.shape[0], rows.shape[1] // 32
    holds = ((2, 0, 8), (3, 0, 8), (1, 0, 8), (0, 0, 8))

    def kernel(mine_ref, z_ref, rows_ref, *refs):
        copies = []
        for (k, begin, count), out in zip(holds, refs):
            member = mine_ref[0] ^ k
            for i in range(count):
                at = lax.rem(z_ref[0] + begin + i, 8)
                start = pl.multiple_of((4 * at + member) * width, width)
                copies.append(
                    pltpu.make_async_copy(
                        rows_ref.at[:, pl.ds(start, width)], out.at[i], refs[-1].at[k, begin + i]
                    )
                )
                copies[-1].start()
        for copy in copies:
            copy.wait()

    over_x, over_both, core, own = pl.pallas_call(
        kernel,
        in_specs=[SMEM, SMEM, pl.BlockSpec(memory_space=pl.ANY)],
        out_specs=[VMEM] * len(holds),
        out_shape=[jax.ShapeDtypeStruct((count, tokens, width), rows.dtype) for _, _, count in holds],
        scratch_shapes=[pltpu.SemaphoreType.DMA((4, 8))],
        compiler_params=pltpu.CompilerParams(vmem_limit_bytes=16 << 20),
    )(mine, z, rows)
    return own, core, over_x, over_both


def tie(value, *others):
    return lax.optimization_barrier((value, *others))[0]


def step(pair, *others):
    pair = lax.optimization_barrier((*pair, *others))
    return lax.ppermute(pair[0], "z", RIGHT), lax.ppermute(pair[1], "z", LEFT)


def ends(pair):
    half = pair[0].shape[0] // 2
    return pair[0][:half], pair[1][half:]


def plus(part, arrived):
    return (part + arrived.astype(F32)).astype(BF16)


def beside(part_of, arrived):
    up, down = arrived
    half = up.shape[0]
    ahead, behind = part_of(3), part_of(-3)
    return (
        jnp.concatenate([plus(ahead[:half], up), ahead[half:].astype(BF16)]),
        jnp.concatenate([behind[:half].astype(BF16), plus(behind[half:], down)]),
    )


def onward(part_of, arrived, d):
    return plus(part_of(d), arrived[0]), plus(part_of(-d), arrived[1])


def side_by_side(*cuts):
    rows = cuts[0][0].shape[0]
    widths = [part.shape[1] for part, _, _ in cuts]
    edges = [sum(widths[:i]) for i in range(len(cuts) + 1)]

    def kernel(*refs):
        for i in range(len(cuts)):
            part, up, down = refs[3 * i : 3 * i + 3]
            refs[-1][:, edges[i] : edges[i + 1]] = part[...] + up[...].astype(F32) + down[...].astype(F32)

    return pl.pallas_call(
        kernel,
        in_specs=[VMEM] * (3 * len(cuts)),
        out_specs=VMEM,
        out_shape=jax.ShapeDtypeStruct((rows, edges[-1]), F32),
        compiler_params=ROOM,
    )(*(array for cut in cuts for array in cut))


def body(activations, inner_weight, out_cotangent, local_fragment, outer_base, outer_momentum):
    weight, fragment = inner_weight[0], local_fragment[0]
    y = lax.axis_index("y")
    mine = lax.axis_index("xh") * 2 + lax.axis_index("c")
    bits = [(y & 2) == 2, (y & 1) == 1, lax.axis_index("xl") == 1]
    weight, activations, fragment, z, mine, *bits = lax.optimization_barrier(
        (weight, activations, fragment, lax.axis_index("z").reshape(1), mine.reshape(1), *bits)
    )

    own_rows, own_columns = outer_base.shape
    stages = ((1, "y", FAR), (2, "y", NEAR), (0, "xl", SWAP))

    def halve(total, stage, *others):
        at, axis, moves = stages[stage]
        low, high = jnp.split(total, 2, axis=at)
        sent = tie(jnp.where(bits[stage], low, high), *others)
        return jnp.where(bits[stage], high, low).astype(F32) + lax.ppermute(sent, axis, moves).astype(F32)

    def double(rows, stage, *others):
        at, axis, moves = stages[stage]
        other = lax.ppermute(tie(rows, *others), axis, moves)
        low, high = jnp.where(bits[stage], other, rows), jnp.where(bits[stage], rows, other)
        return jnp.concatenate([low, high], axis=at)

    def near(shard, one, two, three):
        return [(0, shard)] + [(s * d, p) for d, pair in enumerate((one, two, three), 1) for s, p in zip((-1, 1), pair)]

    def part_with(slopes):
        return lambda d: lax.dot_general(
            blocks[d % 8], slopes, (((0,), (0,)), ((), ())), preferred_element_type=F32
        )

    def slopes_from(own, from_core, from_x, cotangent):
        mine = slopes_of(own, from_core, from_x, cotangent)
        from_both = lax.ppermute(mine, ("xh", "c"), BOTH)
        return jnp.concatenate([mine, lax.ppermute(mine, "xh", SWAP), lax.ppermute(mine, "c", SWAP), from_both])

    shards = cut_columns(weight)
    a1 = step((shards[0], shards[0]))
    own, core, over_x, over_both = split_columns(tie(activations, shards[0]), mine, z)
    from_x = lax.ppermute(over_x, "xh", SWAP)
    from_core = lax.ppermute(core, "c", SWAP)
    b1 = step((shards[1], shards[1]))
    a2, b2 = step(a1), step(b1)
    from_both = lax.ppermute(tie(over_both, from_x), ("xh", "c"), BOTH)
    total = halve(fragment.reshape(2, 2, 2, own_rows, own_columns), 0, *a1)
    a3, b3 = step(a2, from_core, total), step(b2)
    total = halve(total, 1, *a2)
    a4, b4 = step(ends(a3), total), step(ends(b3))

    pieces = (own, from_x, from_core, from_both)
    sums, blocks = project(pieces, (near(shards[0], a1, a2, a3), near(shards[1], b1, b2, b3)))
    partial = complete(sums, blocks[4], (a4, b4))
    crossed = [lax.ppermute(crossing, "c", SWAP) for _, _, crossing in partial]
    arrived = [
        lax.ppermute(plus(over_x, from_core[1]), "xh", SWAP)
        for (_, over_x, _), from_core in zip(partial, crossed)
    ]
    slopes = slopes_from(partial[0][0], crossed[0], arrived[0], out_cotangent[:, :CUT])
    first = part_with(slopes)

    far = first(4).astype(BF16)
    t1 = step(ends((far, far)))
    total = halve(total, 2, *t1)
    slopes = slopes_from(partial[1][0], crossed[1], arrived[1], out_cotangent[:, CUT:])
    second = part_with(slopes)
    far = second(4).astype(BF16)
    u1 = step(ends((far, far)))
    delta = outer_base - total.reshape(own_rows, own_columns) / 8
    new_momentum = 0.9 * outer_momentum + delta
    new_base = outer_base - 0.7 * (delta + 0.9 * new_momentum)
    t2 = step(beside(first, t1))
    half_base = double(new_base.astype(BF16).reshape(1, 1, 1, own_rows, own_columns), 2, *t1)
    u2 = step(beside(second, u1), new_base)
    t3 = step(onward(first, t2, 2), half_base)
    half_base = double(half_base, 1, *t2)
    u3 = step(onward(second, u2, 2))
    t4 = step(onward(first, t3, 1), half_base)
    half_base = double(half_base, 0, *t3)
    u4 = step(onward(second, u3, 1))
    grad = side_by_side((first(0), *t4), (second(0), *u4))
    half_base = half_base.reshape(fragment.shape)
    merged = (0.5 * half_base.astype(F32) + 0.5 * fragment.astype(F32)).astype(BF16)
    return grad[None], new_base, new_momentum, merged[None]


def solution(mesh):
    axes = ("xl", "y", "z", "xh", "c")
    mesh = Mesh(mesh.devices.reshape(2, 4, 8, 2, 2), axes)
    replica, fsdp = ("xl", "y"), ("z", "xh", "c")
    placed = (
        P(axes, None),
        P(replica, fsdp, None),
        P(axes, None),
        P(replica, None, fsdp),
        P(replica, fsdp),
        P(replica, fsdp),
    )
    return jax.shard_map(
        body,
        mesh=mesh,
        in_specs=placed,
        out_specs=(
            P(replica, fsdp, None),
            P(replica, fsdp),
            P(replica, fsdp),
            P(replica, None, fsdp),
        ),
        check_vma=False,
    )
```
